32 devices in a mesh: dp: 4 (over z), expert: 4 (over y, x), tensor: 2 (over core).
Axes of the slice: x: 2, y: 2, z: 4, core: 2. Of those that a mesh axis runs over, the one named last changes fastest.
Arguments:
- hidden_in: bfloat16 [4096, 2048], P(('dp', 'expert')), may hold values from -6 to 6
- query: bfloat16 [4096, 2048], P(('dp', 'expert'), 'tensor'), may hold values from -26 to 26
- keys: bfloat16 [4096, 2048], P(('dp', 'expert'), 'tensor'), may hold values from -26 to 26
- values: bfloat16 [4096, 2048], P(('dp', 'expert'), 'tensor'), may hold values from -6 to 6
- out_proj: bfloat16 [2048, 2048], P('tensor'), may hold values from -0.125 to 0.125
- norm_gain: bfloat16 [2048], replicated, may hold values from 0.25 to 1.75
- routes: int32 [4096, 2], P(('dp', 'expert')), may hold values from 0 to 3, all different within a row; in each aligned block of 256 rows (0 to 255, 256 to 511, ...) at most 144 rows name the same one
- gates: float32 [4096, 2], P(('dp', 'expert')), may hold values from 0.2 to 1
- w_gate: bfloat16 [4, 2048, 5504], P('expert', 'dp', 'tensor'), may hold values from -0.125 to 0.125
- w_up: bfloat16 [4, 2048, 5504], P('expert', 'dp', 'tensor'), may hold values from -0.125 to 0.125
- w_down_t: bfloat16 [4, 2048, 5504], P('expert', 'dp', 'tensor'), may hold values from -0.078125 to 0.078125
Outputs:
- layer_out: bfloat16 [4096, 2048], P(('dp', 'expert'), 'tensor')
The draws below stay inside these ranges and needn't reach their ends.
Inputs may be any that keep to these rules, and one draw needn't show every extreme that they name: `routes`: each row names 2 different experts; in the 256 rows of one block of consecutive tokens no expert is named more than 144 times, a bound that some block reaches.
All inputs are finite; a program needn't handle non-finite values.
Results may differ from the reference program's by a relative error of at most 0.0095.
Values may be sent and summed in bfloat16 or wider, within the bound.
A program may use at most 128 MiB of HBM per device.

```python
import math
import jax
import jax.numpy as jnp
import numpy as np
from jax import lax

D = 2048
HDIM = 128
FF = 5504
TOP = 2
TOK = 256
HEADS = 16
EXPERTS = 4
SEQ = 1024
TOKENS = 4096
CAP = 144
N_TENSOR = 2


def drawn_pair(key):
    key_a, key_b = jax.random.split(jax.random.fold_in(key, 4049), 2)
    query_draw = jax.random.normal(key_a, (TOKENS, D), jnp.float32)
    keys_draw = jax.random.normal(key_b, (TOKENS, D), jnp.float32)
    return (query_draw, keys_draw)


def draw_query(key, part):
    return drawn_pair(key)[0].astype(jnp.bfloat16)


def draw_keys(key, part):
    return drawn_pair(key)[1].astype(jnp.bfloat16)


def shard_levels(key, shape, cuts, smallest, largest):
    def one(position, parts):
        steps = jax.random.uniform(jax.random.fold_in(jax.random.fold_in(key, 6), position), (parts,), jnp.float32, smallest / len(cuts), largest / len(cuts))
        return jnp.repeat(jnp.exp(steps), shape[position] // parts).reshape((-1,) + (1,) * (len(shape) - position - 1))

    factor_of = one(*cuts[0])
    for cut in cuts[1:]:
        factor_of = factor_of * one(*cut)
    return factor_of


def deal_out(key, own, number, rows, count, top, bound, slope):
    ranking = jax.random.permutation(key, count)
    heavy_load, usual = load_shares(count, rows * top, bound, slope, True), load_shares(count, rows * top, bound, slope, False)
    places = jnp.arange(count)

    def named(tallies, rotation):
        used = int((tallies > 0).sum())
        fixed = max(1, used // 4)
        shifted = fixed + (places - fixed + rotation * (used - fixed)) % max(1, count - fixed)
        return jnp.zeros((count,), jnp.int32).at[ranking[jnp.where(places < fixed, places, shifted)]].set(jnp.asarray(tallies, jnp.int32))

    tallies = jnp.where(number % 4 == 0, named(heavy_load, number // 4), named(usual, number - number // 4 - 1))
    mixed = jax.random.permutation(jax.random.fold_in(own, 3), count)
    source_of, sink = mixed[0:count // 2 * 2:2], mixed[1:count // 2 * 2:2]
    margin = jnp.minimum(tallies[source_of] - 1, bound - tallies[sink]) // 2
    margin = jnp.where((source_of == ranking[0]) | (sink == ranking[0]) | (tallies[sink] == 0), 0, jnp.maximum(margin, 0))
    shifted = jax.random.randint(jax.random.fold_in(own, 4), (count // 2,), 0, 1 << 20) % (margin + 1)
    tallies = tallies.at[source_of].add(-shifted).at[sink].add(shifted)
    members = jnp.searchsorted(jnp.cumsum(tallies), jnp.arange(rows * top), side="right").astype(jnp.int32)
    listing = members.reshape(top, rows).T
    listing = listing[jax.random.permutation(jax.random.fold_in(own, 1), rows)]
    rotation = jax.random.randint(jax.random.fold_in(own, 2), (rows, 1), 0, top)
    return jnp.take_along_axis(listing, (jnp.arange(top)[None, :] + rotation) % top, axis=1)


def load_shares(amount, total, limit, skew, full):
    portions = [(1 << 20) // math.isqrt(standing ** skew) + 1 for standing in range(1, amount + 1)]
    largest = limit if full else min(limit, max(-(-total // amount), total * portions[0] // sum(portions)))
    least = 1 if total - largest >= amount - 1 else 0
    holding, rest = [largest] + [least] * (amount - 1), total - largest - least * (amount - 1)
    while rest > 0:
        candidates = [i for i in range(1, amount) if holding[i] < largest] or [i for i in range(1, amount) if holding[i] < limit]
        pool, left = sum([portions[i] for i in candidates]), rest
        for i in candidates:
            addition = min(limit - holding[i], max(1, left * portions[i] // pool), rest)
            holding[i] = holding[i] + addition
            rest = rest - addition
    return np.array(holding)


def bell_draw(stream_key, shape, scale, most, pieces=(), kind=jnp.bfloat16):
    level = shard_levels(stream_key, shape, pieces, -0.22, 0.18) if pieces else 1.0
    values = jax.random.normal(stream_key, shape, jnp.float32) * scale * level
    return jnp.minimum(jnp.maximum(values, -most), most).astype(kind)


def setup_inputs(seed: int = 0) -> dict:
    seeds = jax.random.split(jax.random.key(seed), 12)
    hidden_in = bell_draw(seeds[0], (TOKENS, D), 1.0, 6.0, ((0, 16),))
    query = draw_query(jax.random.fold_in(seeds[11], 71), 0)
    keys = draw_keys(jax.random.fold_in(seeds[11], 71), 0)
    values = bell_draw(seeds[3], (TOKENS, D), 1.0, 6.0, ((0, 16), (1, 2)))
    out_proj = bell_draw(seeds[4], (D, D), D ** -0.5, 0.125, ((0, 2),))
    norm_gain = jnp.clip(1.0 + 0.15 * jax.random.normal(seeds[5], (D,), jnp.float32), 0.25, 1.75).astype(jnp.bfloat16)
    routes_keys = jax.random.split(jax.random.fold_in(seeds[6], 1), TOKENS // TOK)
    routes_turns = jax.random.permutation(jax.random.fold_in(seeds[6], 3), TOKENS // TOK)
    routes = jax.vmap(lambda own, number: deal_out(jax.random.fold_in(seeds[6], 2), own, number, TOK, EXPERTS, TOP, CAP, 2))(routes_keys, routes_turns).reshape((TOKENS, TOP))
    gates = jnp.clip(0.2 + 0.8 * jax.random.uniform(seeds[7], (TOKENS, TOP), jnp.float32) ** shard_levels(seeds[7], (TOKENS, TOP), ((0, 16),), -0.2, 0.2), 0.2, 1.0)
    w_gate = bell_draw(seeds[8], (EXPERTS, D, FF), D ** -0.5, 0.125, ((0, 4), (1, 4), (2, 2)))
    w_up = bell_draw(seeds[9], (EXPERTS, D, FF), D ** -0.5, 0.125, ((0, 4), (1, 4), (2, 2)))
    w_down_t = bell_draw(seeds[10], (EXPERTS, D, FF), FF ** -0.5, 0.078125, ((0, 4), (1, 4), (2, 2)))
    return {"hidden_in": hidden_in, "query": query, "keys": keys, "values": values, "out_proj": out_proj, "norm_gain": norm_gain, "routes": routes, "gates": gates, "w_gate": w_gate, "w_up": w_up, "w_down_t": w_down_t}


EPSILON = 1e-05
NEGATIVE = -1e+30

def slot_table(block_routes, experts, capacity):
    flat_routes = block_routes.reshape(-1).astype(jnp.int32)
    onehot = (flat_routes[:, None] == jnp.arange(experts, dtype=jnp.int32)[None, :]).astype(jnp.int32)
    rank_table = jnp.cumsum(onehot, axis=0) - 1
    slot_index = lax.optimization_barrier(jnp.sum(rank_table * onehot, axis=1))
    return (flat_routes * capacity + slot_index).astype(jnp.int32)

def attend_sequence(packed):
    queries, key_rows, value_rows = packed
    score_scale = 1.0 / HDIM ** 0.5
    queries = queries.astype(jnp.float32).reshape(SEQ, HEADS, HDIM)
    key_rows = key_rows.astype(jnp.float32).reshape(SEQ, HEADS, HDIM)
    value_rows = value_rows.astype(jnp.float32).reshape(SEQ, HEADS, HDIM)
    scores = jnp.einsum('qhd,khd->hqk', queries, key_rows) * score_scale
    causal = (jnp.arange(SEQ)[:, None] >= jnp.arange(SEQ)[None, :])[None]
    scores = jnp.where(causal, scores, NEGATIVE)
    maxima = lax.optimization_barrier(jnp.max(scores, axis=-1, keepdims=True))
    weights = jnp.where(causal, jnp.exp(scores - maxima), 0.0)
    totals = lax.optimization_barrier(jnp.sum(weights, axis=-1))
    context = jnp.einsum('hqk,khd->hqd', weights, value_rows) / totals[..., None]
    return jnp.transpose(context, (1, 0, 2)).reshape(SEQ, HEADS * HDIM)

def reference(hidden_in, query, keys, values, out_proj, norm_gain, routes, gates, w_gate, w_up, w_down_t):
    sequences = TOKENS // SEQ
    context = lax.map(attend_sequence, (query.reshape(sequences, SEQ, D), keys.reshape(sequences, SEQ, D), values.reshape(sequences, SEQ, D)))
    context = context.reshape(TOKENS, D).astype(jnp.bfloat16)
    attended = jnp.dot(context, out_proj, preferred_element_type=jnp.float32)
    residual = hidden_in.astype(jnp.float32) + attended
    mean_square = lax.optimization_barrier(jnp.mean(residual * residual, axis=-1, keepdims=True))
    normed = (residual * lax.rsqrt(mean_square + EPSILON) * norm_gain.astype(jnp.float32)).astype(jnp.bfloat16)
    blocks = TOKENS // TOK

    def block_slots(block_routes):
        return slot_table(block_routes, EXPERTS, CAP)
    targets = jax.vmap(block_slots)(routes.reshape(blocks, TOK, TOP))
    doubled = jnp.repeat(normed.reshape(blocks, TOK, D), TOP, axis=1)
    block_index = jnp.broadcast_to(jnp.arange(blocks, dtype=jnp.int32)[:, None], targets.shape)
    dispatched = jnp.zeros((blocks, EXPERTS * CAP, D), jnp.bfloat16).at[block_index, targets].set(doubled)
    dispatched = jnp.transpose(dispatched.reshape(blocks, EXPERTS, CAP, D), (1, 0, 2, 3)).reshape(EXPERTS, blocks * CAP, D)
    ff_share = FF // N_TENSOR

    def run_expert(packed):
        expert_rows, gate_weights, up_weights, down_weights = packed
        gate_out = jnp.dot(expert_rows, gate_weights, preferred_element_type=jnp.float32)
        up_out = jnp.dot(expert_rows, up_weights, preferred_element_type=jnp.float32)
        hidden = (jax.nn.silu(gate_out) * up_out).astype(jnp.bfloat16)
        summed = jnp.zeros((expert_rows.shape[0], D), jnp.float32)
        for tensor_part in range(N_TENSOR):
            down_term = lax.dot_general(hidden[:, tensor_part * ff_share:(tensor_part + 1) * ff_share], down_weights[:, tensor_part * ff_share:(tensor_part + 1) * ff_share], (((1,), (1,)), ((), ())), preferred_element_type=jnp.float32)
            rounded = lax.optimization_barrier(down_term.astype(jnp.bfloat16))
            summed = summed + rounded.astype(jnp.float32)
        return summed
    results = lax.map(run_expert, (dispatched, w_gate, w_up, w_down_t))
    results = jnp.transpose(results.reshape(EXPERTS, blocks, CAP, D), (1, 0, 2, 3)).reshape(blocks, EXPERTS * CAP, D)
    fetched = results[block_index, targets].reshape(TOKENS, TOP, D)
    mixture = lax.optimization_barrier(jnp.sum(gates[:, :, None] * fetched, axis=1))
    return (residual + mixture).astype(jnp.bfloat16)
```

```python
import jax
import jax.numpy as jnp
from jax import lax
from jax.sharding import PartitionSpec as P

HDIM = 128


EPSILON = 1e-05
NEGATIVE = -1e30


def slot_table(block_routes, experts, capacity):
    flat_routes = block_routes.reshape(-1)
    pairs = flat_routes.shape[0]
    onehot = flat_routes[:, None] == jnp.arange(experts, dtype=jnp.int32)[None, :]
    order = jnp.arange(pairs, dtype=jnp.int32)
    earlier = (order[:, None] > order[None, :]).astype(jnp.bfloat16)
    rank_table = jnp.dot(
        earlier, onehot.astype(jnp.bfloat16), preferred_element_type=jnp.float32
    )
    slot_index = jnp.sum(jnp.where(onehot, rank_table, 0.0), axis=1).astype(jnp.int32)
    return flat_routes * capacity + slot_index


def attention(query, keys, values, score_scale):
    tok_rows, head_cols = query.shape
    head_count = head_cols // HDIM
    query_pos = lax.axis_index("expert") * tok_rows + jnp.arange(tok_rows, dtype=jnp.int32)
    both = lax.all_gather(jnp.concatenate([keys, values], axis=1), "expert", axis=0, tiled=True)
    key_rows, value_rows = both[:, :head_cols], both[:, head_cols:]
    count_rows = key_rows.shape[0]
    key_pos = jnp.arange(count_rows, dtype=jnp.int32)
    queries = query.reshape(tok_rows, head_count, HDIM)
    key_part = key_rows.reshape(count_rows, head_count, HDIM)
    value_part = value_rows.reshape(count_rows, head_count, HDIM)
    scores = (
        jnp.einsum("qhd,khd->hqk", queries, key_part, preferred_element_type=jnp.float32)
        * score_scale
    )
    causal = (query_pos[:, None] >= key_pos[None, :])[None]
    scores = jnp.where(causal, scores, NEGATIVE)
    new_max = jnp.max(scores, axis=-1)
    weights_now = jnp.where(causal, jnp.exp(scores - new_max[..., None]), 0.0)
    totals = jnp.sum(weights_now, axis=-1)
    weighted = jnp.einsum("hqk,khd->hqd", weights_now, value_part.astype(jnp.float32))
    context = weighted / totals[..., None]
    return jnp.transpose(context, (1, 0, 2)).reshape(tok_rows, head_cols).astype(jnp.bfloat16)


def local(
    hidden_in, query, keys, values, out_proj, norm_gain, routes, gates, w_gate, w_up, w_down_t
):
    tok_rows, feature_width = hidden_in.shape
    top = routes.shape[1]
    experts = lax.axis_size("expert")
    copies = lax.axis_size("dp")
    capacity = 9 * tok_rows // (4 * experts)
    slots = experts * capacity
    tensor_count = lax.axis_size("tensor")
    slice_width = feature_width // tensor_count
    tensor_index = lax.axis_index("tensor")
    shard_rows, hidden_width = w_gate.shape[1:]
    exchange = 2 * slots * feature_width < 3 * shard_rows * hidden_width
    if hidden_width % copies:
        exchange = False

    def spread(w):
        if not exchange:
            return lax.all_gather(w[0], "dp", axis=0, tiled=True)
        share = hidden_width // copies
        me = lax.axis_index("dp")
        turned = jnp.transpose(w[0]).reshape(copies, share, shard_rows)
        whole = jnp.zeros((copies, share, shard_rows), w.dtype)
        for step in range(copies):
            block = lax.dynamic_index_in_dim(turned, (me + step) % copies, 0, keepdims=True)
            if step:
                block = lax.ppermute(
                    block, "dp", [(i, (i + step) % copies) for i in range(copies)]
                )
            whole = lax.dynamic_update_slice_in_dim(
                whole, block, (me - step + copies) % copies, 0
            )
        return jnp.transpose(whole, (0, 2, 1)).reshape(copies * shard_rows, share)

    gate_full, up_full, down_full = spread(w_gate), spread(w_up), spread(w_down_t)

    context = attention(query, keys, values, 1.0 / HDIM**0.5)
    attended = lax.psum(
        jnp.dot(context, out_proj, preferred_element_type=jnp.float32).astype(jnp.bfloat16),
        "tensor",
    ).astype(jnp.float32)
    residual = hidden_in.astype(jnp.float32) + attended
    mean_square = jnp.mean(residual * residual, axis=-1, keepdims=True)
    normed = (residual * lax.rsqrt(mean_square + EPSILON) * norm_gain.astype(jnp.float32)).astype(
        jnp.bfloat16
    )
    targets = slot_table(routes, experts, capacity).reshape(tok_rows, top)
    chosen = targets[:, :, None] == jnp.arange(slots, dtype=jnp.int32)[None, None, :]
    place = jnp.any(chosen, axis=1).astype(jnp.bfloat16)
    own_cols = lax.dynamic_slice_in_dim(normed, tensor_index * slice_width, slice_width, 1)
    send_rows = lax.dot_general(
        place, own_cols, (((0,), (0,)), ((), ())), preferred_element_type=jnp.float32
    ).astype(jnp.bfloat16)
    send_rows, gate_full, up_full = lax.optimization_barrier((send_rows, gate_full, up_full))
    arrived = lax.all_to_all(
        send_rows.reshape(experts, capacity, slice_width),
        "expert",
        split_axis=0,
        concat_axis=0,
        tiled=True,
    ).reshape(slots, slice_width)
    if exchange:
        arrived, down_full = lax.optimization_barrier((arrived, down_full))
        arrived = lax.all_gather(arrived, "dp", axis=0, tiled=True)
    halves = lax.all_gather(arrived, "tensor", axis=0)
    slot_rows = jnp.concatenate([halves[i] for i in range(tensor_count)], axis=1)
    gate_out = jnp.dot(slot_rows, gate_full, preferred_element_type=jnp.float32)
    up_out = jnp.dot(slot_rows, up_full, preferred_element_type=jnp.float32)
    hidden = (jax.nn.silu(gate_out) * up_out).astype(jnp.bfloat16)
    rounded = lax.dot_general(
        hidden, down_full, (((1,), (1,)), ((), ())), preferred_element_type=jnp.float32
    ).astype(jnp.bfloat16)
    own_slice = lax.dynamic_slice_in_dim(residual, tensor_index * slice_width, slice_width, 1)
    summed = lax.psum_scatter(rounded, "tensor", scatter_dimension=1, tiled=True)
    if exchange:
        summed = lax.psum_scatter(summed, "dp", scatter_dimension=0, tiled=True)
    returned = lax.all_to_all(
        summed.reshape(experts, capacity, slice_width),
        "expert",
        split_axis=0,
        concat_axis=0,
        tiled=True,
    ).reshape(slots, slice_width)
    mixing = jnp.sum(jnp.where(chosen, gates[:, :, None], 0.0), axis=1)
    mixture = jnp.dot(
        mixing,
        returned.astype(jnp.float32),
        precision=lax.Precision.HIGHEST,
        preferred_element_type=jnp.float32,
    )
    return (own_slice + mixture).astype(jnp.bfloat16)


def solution(mesh):
    in_specs = (
        P(("dp", "expert"), None),
        P(("dp", "expert"), "tensor"),
        P(("dp", "expert"), "tensor"),
        P(("dp", "expert"), "tensor"),
        P("tensor", None),
        P(),
        P(("dp", "expert"), None),
        P(("dp", "expert"), None),
        P("expert", "dp", "tensor"),
        P("expert", "dp", "tensor"),
        P("expert", "dp", "tensor"),
    )
    out_specs = P(("dp", "expert"), "tensor")
    return jax.shard_map(local, mesh=mesh, in_specs=in_specs, out_specs=out_specs, check_vma=False)
```

```python
import jax
import jax.numpy as jnp
from jax import lax
from jax.sharding import PartitionSpec as P

HDIM = 128


EPSILON = 1e-05
NEGATIVE = -1e30


def slot_table(block_routes, experts, capacity):
    flat_routes = block_routes.reshape(-1)
    pairs = flat_routes.shape[0]
    onehot = flat_routes[:, None] == jnp.arange(experts, dtype=jnp.int32)[None, :]
    order = jnp.arange(pairs, dtype=jnp.int32)
    earlier = (order[:, None] > order[None, :]).astype(jnp.bfloat16)
    rank_table = jnp.dot(
        earlier, onehot.astype(jnp.bfloat16), preferred_element_type=jnp.float32
    )
    slot_index = jnp.sum(jnp.where(onehot, rank_table, 0.0), axis=1).astype(jnp.int32)
    return flat_routes * capacity + slot_index


def attention(query, both, score_scale):
    tok_rows, head_cols = query.shape
    head_count = head_cols // HDIM
    query_pos = lax.axis_index("expert") * tok_rows + jnp.arange(tok_rows, dtype=jnp.int32)
    key_rows, value_rows = both[:, :head_cols], both[:, head_cols:]
    count_rows = key_rows.shape[0]
    key_pos = jnp.arange(count_rows, dtype=jnp.int32)
    queries = query.reshape(tok_rows, head_count, HDIM)
    key_part = key_rows.reshape(count_rows, head_count, HDIM)
    value_part = value_rows.reshape(count_rows, head_count, HDIM)
    scores = (
        jnp.einsum("qhd,khd->hqk", queries, key_part, preferred_element_type=jnp.float32)
        * score_scale
    )
    causal = (query_pos[:, None] >= key_pos[None, :])[None]
    scores = jnp.where(causal, scores, NEGATIVE)
    new_max = jnp.max(scores, axis=-1)
    weights_now = jnp.where(causal, jnp.exp(scores - new_max[..., None]), 0.0)
    totals = jnp.sum(weights_now, axis=-1)
    weighted = jnp.einsum("hqk,khd->hqd", weights_now, value_part.astype(jnp.float32))
    context = weighted / totals[..., None]
    return jnp.transpose(context, (1, 0, 2)).reshape(tok_rows, head_cols).astype(jnp.bfloat16)


def local(
    hidden_in, query, keys, values, out_proj, norm_gain, routes, gates, w_gate, w_up, w_down_t
):
    tok_rows, feature_width = hidden_in.shape
    top = routes.shape[1]
    experts = lax.axis_size("expert")
    copies = lax.axis_size("dp")
    capacity = 9 * tok_rows // (4 * experts)
    slots = experts * capacity
    tensor_count = lax.axis_size("tensor")
    slice_width = feature_width // tensor_count
    tensor_index = lax.axis_index("tensor")
    shard_rows, hidden_width = w_gate.shape[1:]
    exchange = 2 * tok_rows * feature_width < 3 * shard_rows * hidden_width and copies <= 4
    if hidden_width % copies:
        exchange = False

    def spread(w):
        if not exchange:
            return lax.all_gather(w[0], "dp", axis=0, tiled=True)
        share = hidden_width // copies
        me = lax.axis_index("dp")
        turned = jnp.transpose(w[0]).reshape(copies, share, shard_rows)
        blocks = []
        for step in range(copies):
            block = lax.dynamic_index_in_dim(turned, (me + step) % copies, 0, keepdims=False)
            if step:
                block = lax.ppermute(
                    block, "dp", [(i, (i + step) % copies) for i in range(copies)]
                )
            blocks.append(block)
        stacked = jnp.stack(blocks)
        ordered = [
            lax.dynamic_index_in_dim(stacked, (me - i + copies) % copies, 0, keepdims=False)
            for i in range(copies)
        ]
        return jnp.transpose(jnp.concatenate(ordered, axis=1))

    gate_full, up_full, down_full = spread(w_gate), spread(w_up), spread(w_down_t)

    choice = jnp.concatenate([routes.astype(jnp.float32), gates], axis=1)
    both = lax.all_gather(jnp.concatenate([keys, values], axis=1), "expert", axis=0, tiled=True)
    if exchange:
        choice = lax.all_gather(choice, "dp", axis=0)
        both, choice, gate_full = lax.optimization_barrier((both, choice, gate_full))
    else:
        choice = choice[None]
    context = attention(query, both, 1.0 / HDIM**0.5)
    attended = lax.psum(
        jnp.dot(context, out_proj, preferred_element_type=jnp.float32).astype(jnp.bfloat16),
        "tensor",
    )
    if exchange:
        attended, up_full = lax.optimization_barrier((attended, up_full))
    attended = attended.astype(jnp.float32)
    residual = hidden_in.astype(jnp.float32) + attended
    mean_square = jnp.mean(residual * residual, axis=-1, keepdims=True)
    normed = (residual * lax.rsqrt(mean_square + EPSILON) * norm_gain.astype(jnp.float32)).astype(
        jnp.bfloat16
    )
    own_cols = lax.dynamic_slice_in_dim(normed, tensor_index * slice_width, slice_width, 1)
    own_slice = lax.dynamic_slice_in_dim(residual, tensor_index * slice_width, slice_width, 1)
    blocks = lax.all_gather(own_cols, "dp", axis=0) if exchange else own_cols[None]
    count = blocks.shape[0]
    sends, mixers = [], []
    slot_numbers = jnp.arange(slots, dtype=jnp.int32)[:, None]
    for i in range(count):
        picked = choice[i, :, :top].astype(jnp.int32)
        targets = slot_table(picked, experts, capacity).reshape(tok_rows, top)
        place = jnp.zeros((slots, tok_rows), jnp.float32)
        mixing = jnp.zeros((slots, tok_rows), jnp.float32)
        for k in range(top):
            chosen = slot_numbers == targets[:, k][None, :]
            place = jnp.where(chosen, 1.0, place)
            mixing = jnp.where(chosen, choice[i, :, top + k][None, :], mixing)
        sent = jnp.dot(
            place.astype(jnp.bfloat16), blocks[i], preferred_element_type=jnp.float32
        ).astype(jnp.bfloat16)
        sends.append(sent.reshape(experts, capacity, slice_width))
        mixers.append(mixing)
    arrived = lax.all_to_all(
        jnp.concatenate(sends, axis=1), "expert", split_axis=0, concat_axis=0, tiled=True
    ).reshape(count * slots, slice_width)
    if exchange:
        arrived, down_full = lax.optimization_barrier((arrived, down_full))
    halves = lax.all_gather(arrived, "tensor", axis=0)
    slot_rows = jnp.concatenate([halves[i] for i in range(tensor_count)], axis=1)
    gate_out = jnp.dot(slot_rows, gate_full, preferred_element_type=jnp.float32)
    up_out = jnp.dot(slot_rows, up_full, preferred_element_type=jnp.float32)
    hidden = (jax.nn.silu(gate_out) * up_out).astype(jnp.bfloat16)
    rounded = lax.dot_general(
        hidden, down_full, (((1,), (1,)), ((), ())), preferred_element_type=jnp.float32
    ).astype(jnp.bfloat16)
    summed = lax.psum_scatter(rounded, "tensor", scatter_dimension=1, tiled=True)
    returned = lax.all_to_all(
        summed.reshape(experts, count * capacity, slice_width),
        "expert",
        split_axis=0,
        concat_axis=0,
        tiled=True,
    )
    mixtures = []
    for i in range(count):
        rows = returned[:, i * capacity : (i + 1) * capacity].reshape(slots, slice_width)
        high = lax.reduce_precision(mixers[i], 8, 7)
        mixtures.append(
            sum(
                lax.dot_general(
                    term.astype(jnp.bfloat16),
                    rows,
                    (((0,), (0,)), ((), ())),
                    preferred_element_type=jnp.float32,
                )
                for term in (high, mixers[i] - high)
            )
        )
    if exchange:
        mixture = lax.psum_scatter(
            jnp.concatenate(mixtures, axis=0).astype(jnp.bfloat16),
            "dp",
            scatter_dimension=0,
            tiled=True,
        ).astype(jnp.float32)
    else:
        mixture = mixtures[0]
    return (own_slice + mixture).astype(jnp.bfloat16)


def solution(mesh):
    in_specs = (
        P(("dp", "expert"), None),
        P(("dp", "expert"), "tensor"),
        P(("dp", "expert"), "tensor"),
        P(("dp", "expert"), "tensor"),
        P("tensor", None),
        P(),
        P(("dp", "expert"), None),
        P(("dp", "expert"), None),
        P("expert", "dp", "tensor"),
        P("expert", "dp", "tensor"),
        P("expert", "dp", "tensor"),
    )
    out_specs = P(("dp", "expert"), "tensor")
    return jax.shard_map(local, mesh=mesh, in_specs=in_specs, out_specs=out_specs, check_vma=False)
```

```python
import jax
import jax.numpy as jnp
from jax import lax
from jax.sharding import PartitionSpec as P

HDIM = 128


EPSILON = 1e-05
NEGATIVE = -1e30


def slot_table(block_routes, experts, capacity):
    flat_routes = block_routes.reshape(-1)
    pairs = flat_routes.shape[0]
    onehot = flat_routes[:, None] == jnp.arange(experts, dtype=jnp.int32)[None, :]
    order = jnp.arange(pairs, dtype=jnp.int32)
    earlier = (order[:, None] > order[None, :]).astype(jnp.bfloat16)
    rank_table = jnp.dot(
        earlier, onehot.astype(jnp.bfloat16), preferred_element_type=jnp.float32
    )
    slot_index = jnp.sum(jnp.where(onehot, rank_table, 0.0), axis=1).astype(jnp.int32)
    return flat_routes * capacity + slot_index


def attention(query, both, score_scale):
    tok_rows, head_cols = query.shape
    head_count = head_cols // HDIM
    query_pos = lax.axis_index("expert") * tok_rows + jnp.arange(tok_rows, dtype=jnp.int32)
    key_rows, value_rows = both[:, :head_cols], both[:, head_cols:]
    count_rows = key_rows.shape[0]
    key_pos = jnp.arange(count_rows, dtype=jnp.int32)
    queries = query.reshape(tok_rows, head_count, HDIM)
    key_part = key_rows.reshape(count_rows, head_count, HDIM)
    value_part = value_rows.reshape(count_rows, head_count, HDIM)
    scores = (
        jnp.einsum("qhd,khd->hqk", queries, key_part, preferred_element_type=jnp.float32)
        * score_scale
    )
    causal = (query_pos[:, None] >= key_pos[None, :])[None]
    scores = jnp.where(causal, scores, NEGATIVE)
    new_max = jnp.max(scores, axis=-1)
    weights_now = jnp.where(causal, jnp.exp(scores - new_max[..., None]), 0.0)
    totals = jnp.sum(weights_now, axis=-1)
    weighted = jnp.einsum("hqk,khd->hqd", weights_now, value_part.astype(jnp.float32))
    context = weighted / totals[..., None]
    return jnp.transpose(context, (1, 0, 2)).reshape(tok_rows, head_cols).astype(jnp.bfloat16)


def local(
    hidden_in, query, keys, values, out_proj, norm_gain, routes, gates, w_gate, w_up, w_down_t
):
    tok_rows, feature_width = hidden_in.shape
    top = routes.shape[1]
    experts = lax.axis_size("expert")
    copies = lax.axis_size("dp")
    capacity = 9 * tok_rows // (4 * experts)
    slots = experts * capacity
    tensor_count = lax.axis_size("tensor")
    slice_width = feature_width // tensor_count
    tensor_index = lax.axis_index("tensor")
    shard_rows, hidden_width = w_gate.shape[1:]
    exchange = 2 * tok_rows * feature_width < 3 * shard_rows * hidden_width and copies <= 4
    if hidden_width % copies:
        exchange = False

    def spread(w):
        if not exchange:
            return lax.all_gather(w[0], "dp", axis=0, tiled=True)
        share = hidden_width // copies
        me = lax.axis_index("dp")
        turned = jnp.transpose(w[0]).reshape(copies, share, shard_rows)
        blocks = []
        for step in range(copies):
            block = lax.dynamic_index_in_dim(turned, (me + step) % copies, 0, keepdims=False)
            if step:
                block = lax.ppermute(
                    block, "dp", [(i, (i + step) % copies) for i in range(copies)]
                )
            blocks.append(block)
        stacked = jnp.stack(blocks)
        ordered = [
            lax.dynamic_index_in_dim(stacked, (me - i + copies) % copies, 0, keepdims=False)
            for i in range(copies)
        ]
        return jnp.transpose(jnp.concatenate(ordered, axis=1))

    choice = jnp.concatenate([routes.astype(jnp.float32), gates], axis=1)
    both = lax.all_gather(jnp.concatenate([keys, values], axis=1), "expert", axis=0, tiled=True)
    if exchange:
        choice = lax.all_gather(choice, "dp", axis=0)
        choice, w_gate, w_up, w_down_t = lax.optimization_barrier(
            (choice, w_gate, w_up, w_down_t)
        )
    else:
        choice = choice[None]
    gate_full, up_full, down_full = spread(w_gate), spread(w_up), spread(w_down_t)
    if exchange:
        both, gate_full = lax.optimization_barrier((both, gate_full))
    context = attention(query, both, 1.0 / HDIM**0.5)
    attended = lax.psum(
        jnp.dot(context, out_proj, preferred_element_type=jnp.float32).astype(jnp.bfloat16),
        "tensor",
    )
    if exchange:
        attended, up_full = lax.optimization_barrier((attended, up_full))
    attended = attended.astype(jnp.float32)
    residual = hidden_in.astype(jnp.float32) + attended
    mean_square = jnp.mean(residual * residual, axis=-1, keepdims=True)
    normed = (residual * lax.rsqrt(mean_square + EPSILON) * norm_gain.astype(jnp.float32)).astype(
        jnp.bfloat16
    )
    own_cols = lax.dynamic_slice_in_dim(normed, tensor_index * slice_width, slice_width, 1)
    own_slice = lax.dynamic_slice_in_dim(residual, tensor_index * slice_width, slice_width, 1)
    blocks = lax.all_gather(own_cols, "dp", axis=0) if exchange else own_cols[None]
    count = blocks.shape[0]
    sends, mixers = [], []
    slot_numbers = jnp.arange(slots, dtype=jnp.int32)[:, None]
    for i in range(count):
        picked = choice[i, :, :top].astype(jnp.int32)
        targets = slot_table(picked, experts, capacity).reshape(tok_rows, top)
        place = jnp.zeros((slots, tok_rows), jnp.float32)
        mixing = jnp.zeros((slots, tok_rows), jnp.float32)
        for k in range(top):
            chosen = slot_numbers == targets[:, k][None, :]
            place = jnp.where(chosen, 1.0, place)
            mixing = jnp.where(chosen, choice[i, :, top + k][None, :], mixing)
        sent = jnp.dot(
            place.astype(jnp.bfloat16), blocks[i], preferred_element_type=jnp.float32
        ).astype(jnp.bfloat16)
        sends.append(sent.reshape(experts, capacity, slice_width))
        mixers.append(mixing)
    arrived = lax.all_to_all(
        jnp.concatenate(sends, axis=1), "expert", split_axis=0, concat_axis=0, tiled=True
    ).reshape(count * slots, slice_width)
    if exchange:
        arrived, down_full = lax.optimization_barrier((arrived, down_full))
    halves = lax.all_gather(arrived, "tensor", axis=0)
    slot_rows = jnp.concatenate([halves[i] for i in range(tensor_count)], axis=1)
    gate_out = jnp.dot(slot_rows, gate_full, preferred_element_type=jnp.float32)
    up_out = jnp.dot(slot_rows, up_full, preferred_element_type=jnp.float32)
    hidden = (jax.nn.silu(gate_out) * up_out).astype(jnp.bfloat16)
    hidden = lax.optimization_barrier(hidden)
    parts = 2 if slice_width % 256 == 0 else 1
    width = slice_width // parts
    down_parts = down_full.reshape(tensor_count, parts, width, down_full.shape[1])
    splits = [(mixing, lax.reduce_precision(mixing, 8, 7)) for mixing in mixers]
    pieces = []
    for part in range(parts):
        rounded = lax.dot_general(
            hidden,
            down_parts[:, part].reshape(tensor_count * width, down_full.shape[1]),
            (((1,), (1,)), ((), ())),
            preferred_element_type=jnp.float32,
        ).astype(jnp.bfloat16)
        summed = lax.psum_scatter(rounded, "tensor", scatter_dimension=1, tiled=True)
        returned = lax.all_to_all(
            summed.reshape(experts, count * capacity, width),
            "expert",
            split_axis=0,
            concat_axis=0,
            tiled=True,
        )
        mixtures = []
        for i, (mixing, high) in enumerate(splits):
            rows = returned[:, i * capacity : (i + 1) * capacity].reshape(slots, width)
            mixtures.append(
                sum(
                    lax.dot_general(
                        term.astype(jnp.bfloat16),
                        rows,
                        (((0,), (0,)), ((), ())),
                        preferred_element_type=jnp.float32,
                    )
                    for term in (high, mixing - high)
                )
            )
        if exchange:
            piece = lax.psum_scatter(
                jnp.concatenate(mixtures, axis=0).astype(jnp.bfloat16),
                "dp",
                scatter_dimension=0,
                tiled=True,
            ).astype(jnp.float32)
        else:
            piece = mixtures[0]
        pieces.append(piece)
    mixture = jnp.concatenate(pieces, axis=1)
    return (own_slice + mixture).astype(jnp.bfloat16)


def solution(mesh):
    in_specs = (
        P(("dp", "expert"), None),
        P(("dp", "expert"), "tensor"),
        P(("dp", "expert"), "tensor"),
        P(("dp", "expert"), "tensor"),
        P("tensor", None),
        P(),
        P(("dp", "expert"), None),
        P(("dp", "expert"), None),
        P("expert", "dp", "tensor"),
        P("expert", "dp", "tensor"),
        P("expert", "dp", "tensor"),
    )
    out_specs = P(("dp", "expert"), "tensor")
    return jax.shard_map(local, mesh=mesh, in_specs=in_specs, out_specs=out_specs, check_vma=False)
```
